512 devices in a mesh: dp: 16 (over x, y_lo), pipe: 8 (over z), expert: 4 (over y_hi, core).
Axes of the slice: x: 4, y: 8 (y_hi: 2, y_lo: 4; y = y_hi * 4 + y_lo), z: 8, core: 2. Of those that a mesh axis runs over, the one named last changes fastest.
Arguments:
- activations: bfloat16 [16, 8, 2, 384, 7168], P('dp', 'pipe', None, None, 'expert'), may hold values from -6 to 6
- out_grads: bfloat16 [16, 8, 2, 384, 576], P('dp', 'pipe', None, 'expert'), may hold values from -0.119628906 to 0.119628906
- counts: int32 [16, 8, 2], P('dp', 'pipe'), may hold values from 96 to 384, as said below
- first_moment: float32 [8, 4, 1792, 576], P('pipe', 'expert', 'dp'), may hold values from -1.8 to 1.8
- second_moment: float32 [8, 4, 1792, 576], P('pipe', 'expert', 'dp'), may hold values from 0.05 to 2
Outputs:
- new_first: float32 [8, 4, 1792, 576], P('pipe', 'expert', 'dp')
- new_second: float32 [8, 4, 1792, 576], P('pipe', 'expert', 'dp')
- direction: float32 [8, 4, 1792, 576], P('pipe', 'expert', 'dp')
The draws below stay inside these ranges and needn't reach their ends.
Inputs may be any that keep to these rules, and one draw needn't show every extreme that they name: `counts`: some span holds 384 live tokens and some span 384 / 4.
All inputs are finite; a program needn't handle non-finite values.
Results may differ from the reference program's by a relative error of at most 0.0003.
Values may be sent and summed in bfloat16 or wider, within the bound.
No kernel may reach another device: no remote copies, remote signals or barrier semaphores. Data moves between devices by JAX's collectives and lax.ppermute only.
A program may use at most 64 MiB of HBM per device.

```python
import math
import jax
import jax.numpy as jnp
from jax import lax

D = 7168
F = 576
MB = 384
N_DP = 16
N_PIPE = 8
N_EXPERT = 4


def draw_counts(key, part):
    key = jax.random.fold_in(key, 5)
    drawn = jax.random.randint(key, (N_DP, N_PIPE, 2), MB // 4, MB + 1, dtype=jnp.int32)
    drawn = drawn.at[0, 0, 0].set(MB)
    drawn = drawn.at[0, 0, 1].set(MB // 4)
    return drawn.astype(jnp.int32)


def shard_levels(rng, shape, pieces, least, high):
    def one(dim, shards_of):
        draws = jax.random.uniform(jax.random.fold_in(jax.random.fold_in(rng, 6), dim), (shards_of,), jnp.float32, least / len(pieces), high / len(pieces))
        return jnp.repeat(jnp.exp(draws), shape[dim] // shards_of).reshape((-1,) + (1,) * (len(shape) - dim - 1))

    level = one(*pieces[0])
    for cut in pieces[1:]:
        level = level * one(*cut)
    return level


def noise(stream_key, extent, scale, bound, shards=(), kind=jnp.bfloat16):
    result = jax.random.normal(stream_key, extent, jnp.float32) * scale
    if len(shards) > 0:
        result = shard_levels(stream_key, extent, shards, -0.22, 0.18) * result
    return jnp.clip(result, min=-bound, max=bound).astype(kind)


def setup_inputs(seed: int = 0) -> dict:
    keys = jax.random.split(jax.random.key(seed), 6)
    return {
        "activations": noise(keys[0], (N_DP, N_PIPE, 2, MB, D), 1.0, 6.0, ((0, 16), (1, 8), (4, 4))),
        "out_grads": noise(keys[1], (N_DP, N_PIPE, 2, MB, F), 0.02, 0.119628906, ((0, 16), (1, 8), (3, 4))),
        "counts": draw_counts(jax.random.fold_in(keys[5], 71), 0),
        "first_moment": noise(keys[3], (N_PIPE, N_EXPERT, D // N_EXPERT, F), 0.3, 1.8, ((0, 8), (1, 4), (2, 16)), jnp.float32),
        "second_moment": jnp.clip(jnp.exp(math.log(2.0) - 3.6888794 * jax.random.uniform(keys[4], (N_PIPE, N_EXPERT, D // N_EXPERT, F), jnp.float32) ** shard_levels(keys[4], (N_PIPE, N_EXPERT, D // N_EXPERT, F), ((0, 8), (1, 4), (2, 16)), -0.2, 0.2)), 0.05, 2.0),
    }


def reference(activations, out_grads, counts, first_moment, second_moment):
    slots = lax.broadcasted_iota(jnp.int32, (N_DP, N_PIPE, 2, MB), 3)
    live = slots < counts[:, :, :, None]
    masked = jnp.where(live[..., None], out_grads, jnp.zeros_like(out_grads))

    def span_part(section, span):
        zero = section * 0
        acts = lax.dynamic_slice(activations, (zero, section, span, zero, zero), (N_DP, 1, 1, MB, D))[:, 0, 0]
        grads = lax.dynamic_slice(masked, (zero, section, span, zero, zero), (N_DP, 1, 1, MB, F))[:, 0, 0]
        return jnp.einsum('btd,btf->bdf', acts.astype(jnp.float32), grads.astype(jnp.float32))

    def section_grad(section):
        own_part = span_part(section, section * 0)
        other_part = span_part((N_PIPE - 1 - section).astype(jnp.int32), section * 0 + 1)
        return lax.optimization_barrier(jnp.sum(own_part + other_part, axis=0))
    grad = lax.map(section_grad, jnp.arange(N_PIPE, dtype=jnp.int32))
    grad = grad.reshape(N_PIPE, N_EXPERT, D // N_EXPERT, F)
    new_first = 0.9 * first_moment + 0.1 * grad
    new_second = 0.95 * second_moment + 0.05 * grad * grad
    direction = new_first / (jnp.sqrt(new_second) + 1e-08)
    return (new_first, new_second, direction)
```

```python
import jax
import jax.numpy as jnp
from jax import lax
from jax.experimental import pallas as pl
from jax.experimental.pallas import tpu as pltpu
from jax.sharding import PartitionSpec as P

AXES = ("dp", "pipe", "expert")
NX, NY = 4, 4
TILE = 256
X_SCALE, Z_SCALE, Y_SCALE = 64.0, 32.0, 16.0


def over_x(step):
    return lambda dp, pipe, expert: ((dp // NY + step) % NX * NY + dp % NY, pipe, expert)


def over_y(bits):
    return lambda dp, pipe, expert: (dp ^ bits, pipe, expert)


def mirrored(dp, pipe, expert):
    return dp, lax.axis_size("pipe") - 1 - pipe, expert


def send(block, to, core):
    sizes = [lax.axis_size(name) for name in AXES]

    def flat(dp, pipe, expert):
        return (dp * sizes[1] + pipe) * sizes[2] + expert

    pairs = [
        (flat(d, p, e), flat(*to(d, p, e)))
        for d in range(sizes[0])
        for p in range(sizes[1])
        for e in range(sizes[2])
        if e % 2 == core
    ]
    return lax.ppermute(block, AXES, pairs)


def transposed_dot(a, b):
    return lax.dot_general(a, b, (((0,), (0,)), ((), ())), preferred_element_type=jnp.float32)


def spans_kernel(counts, acts, grads, own, other, masked_other, masked):
    @pl.when(pl.program_id(0) == 0)
    def _():
        slots = lax.broadcasted_iota(jnp.int32, masked.shape[1:], 0)
        for span in range(2):
            live = slots < counts[span]
            kept = jnp.where(live, grads[span].astype(jnp.float32), 0.0).astype(masked.dtype)
            masked[span] = kept
        masked_other[...] = masked[1]

    own[...] = transposed_dot(acts[0, 0, 0], masked[0])
    other[...] = transposed_dot(acts[0, 0, 1], masked[1])


def both_spans(counts, activations, grads):
    _, _, spans, slots, rows = activations.shape
    width = grads.shape[-1]
    part = jax.ShapeDtypeStruct((rows, width), jnp.float32)
    return pl.pallas_call(
        spans_kernel,
        grid_spec=pltpu.PrefetchScalarGridSpec(
            num_scalar_prefetch=1,
            grid=(rows // TILE,),
            in_specs=[
                pl.BlockSpec((1, 1, spans, slots, TILE), lambda i, c: (0, 0, 0, 0, i)),
                pl.BlockSpec((spans, slots, width), lambda i, c: (0, 0, 0)),
            ],
            out_specs=[
                pl.BlockSpec((TILE, width), lambda i, c: (i, 0)),
                pl.BlockSpec((TILE, width), lambda i, c: (i, 0)),
                pl.BlockSpec((slots, width), lambda i, c: (0, 0)),
            ],
            scratch_shapes=[pltpu.VMEM((spans, slots, width), grads.dtype)],
        ),
        out_shape=[part, part, jax.ShapeDtypeStruct((slots, width), grads.dtype)],
        compiler_params=pltpu.CompilerParams(vmem_limit_bytes=32 << 20),
        cost_estimate=pl.CostEstimate(
            flops=4 * slots * rows * width, bytes_accessed=12 << 20, transcendentals=0
        ),
    )(counts, activations, grads)


def mirror_kernel(acts, grads, base, total):
    total[...] = base[...] + transposed_dot(acts[...], grads[...])


def add_mirror(acts, grads, base):
    slots, rows = acts.shape
    width = grads.shape[-1]
    return pl.pallas_call(
        mirror_kernel,
        grid=(rows // TILE,),
        in_specs=[
            pl.BlockSpec((slots, TILE), lambda i: (0, i)),
            pl.BlockSpec((slots, width), lambda i: (0, 0)),
            pl.BlockSpec((TILE, width), lambda i: (i, 0)),
        ],
        out_specs=pl.BlockSpec((TILE, width), lambda i: (i, 0)),
        out_shape=jax.ShapeDtypeStruct((rows, width), jnp.float32),
        compiler_params=pltpu.CompilerParams(vmem_limit_bytes=32 << 20),
        cost_estimate=pl.CostEstimate(
            flops=2 * slots * rows * width, bytes_accessed=11 << 20, transcendentals=0
        ),
    )(acts, grads, base)


def piece(array, index, pieces):
    rows = array.shape[0] // pieces
    return lax.dynamic_slice_in_dim(array, index * rows, rows, 0)


def narrow(values, scale):
    return (values * scale).astype(jnp.float16)


def widen(values, scale):
    return values.astype(jnp.float32) * (1.0 / scale)


def exchange_x(part, x, core):
    return [
        send(narrow(piece(part, (x + k) % NX, NX), X_SCALE), over_x(k), core)
        for k in range(1, NX)
    ]


def exchange_y(part, y, core):
    return [
        send(narrow(piece(part, y ^ k, NY), Y_SCALE), over_y(k), core) for k in range(1, NY)
    ]


def collect(own, received, scale):
    for block in received:
        own = own + widen(block, scale)
    return own


def local(activations, out_grads, counts, first_moment, second_moment):
    dp = lax.axis_index("dp")
    core = lax.axis_index("expert") % 2
    x, y = dp // NY, dp % NY
    mirror_acts = send(activations[0, 0, 1], mirrored, 0)
    grads = lax.all_gather(out_grads[0, 0], "expert", axis=1, tiled=True)
    own, other, masked_other = both_spans(counts[0, 0], activations, grads)
    mirror_grads = send(masked_other, mirrored, 0)

    other_x = collect(piece(other, x, NX), exchange_x(other, x, 1), X_SCALE)
    own_in = exchange_x(own, x, 1)
    other_z = send(narrow(other_x, Z_SCALE), mirrored, 1)
    quarter_1 = collect(piece(own, x, NX), own_in, X_SCALE) + widen(other_z, Z_SCALE)
    last_1 = exchange_y(quarter_1, y, 1)

    both = add_mirror(mirror_acts, mirror_grads, own)
    quarter_0 = collect(piece(both, x, NX), exchange_x(both, x, 0), X_SCALE)
    last_0 = exchange_y(quarter_0, y, 0)

    rows_1 = collect(piece(quarter_1, y, NY), last_1, Y_SCALE)
    rows_0 = collect(piece(quarter_0, y, NY), last_0, Y_SCALE)
    grad = jnp.where(core == 1, rows_1, rows_0)[None, None]
    new_first = 0.9 * first_moment + 0.1 * grad
    new_second = 0.95 * second_moment + 0.05 * grad * grad
    direction = new_first / (jnp.sqrt(new_second) + 1e-08)
    return (new_first, new_second, direction)


def solution(mesh):
    state = P("pipe", "expert", "dp", None)
    return jax.shard_map(
        local,
        mesh=mesh,
        in_specs=(
            P("dp", "pipe", None, None, "expert"),
            P("dp", "pipe", None, "expert", None),
            P("dp", "pipe", None),
            state,
            state,
        ),
        out_specs=(state, state, state),
        check_vma=False,
    )
```

```python
import functools

import jax
import jax.numpy as jnp
from jax import lax
from jax.experimental import pallas as pl
from jax.experimental.pallas import tpu as pltpu
from jax.sharding import PartitionSpec as P

AXES = ("dp", "pipe", "expert")
NX, NY = 4, 4
X_SCALE, Y_SCALE, Z_SCALE = 64.0, 32.0, 8.0
VMEM_BYTES = 32 << 20


def first_step(expert):
    return 1 + 2 * (expert % 2)


def over_x_first(dp, pipe, expert):
    return dp ^ first_step(expert) * NY, pipe, expert


def over_x_second(dp, pipe, expert):
    return dp ^ (4 - first_step(expert)) * NY, pipe, expert


def over_y(bits):
    return lambda dp, pipe, expert: (dp ^ bits, pipe, expert)


def mirrored(dp, pipe, expert):
    return dp, lax.axis_size("pipe") - 1 - pipe, expert


def send(block, to):
    sizes = [lax.axis_size(name) for name in AXES]

    def flat(dp, pipe, expert):
        return (dp * sizes[1] + pipe) * sizes[2] + expert

    pairs = [
        (flat(d, p, e), flat(*to(d, p, e)))
        for d in range(sizes[0])
        for p in range(sizes[1])
        for e in range(sizes[2])
    ]
    return lax.ppermute(block, AXES, pairs)


def transposed_dot(a, b):
    return lax.dot_general(a, b, (((0,), (0,)), ((), ())), preferred_element_type=jnp.float32)


def cost(flops, read_and_written):
    return pl.CostEstimate(flops=flops, bytes_accessed=read_and_written, transcendentals=0)


def span_kernel(span, counts, acts, grads, part, masked):
    @pl.when(pl.program_id(0) == 0)
    def _():
        live = lax.broadcasted_iota(jnp.int32, masked.shape, 0) < counts[span]
        masked[...] = jnp.where(live, grads[0].astype(jnp.float32), 0.0).astype(masked.dtype)

    product = transposed_dot(acts[0, 0, 0], masked[...])
    x = lax.axis_index("dp") // NY
    first = first_step(lax.axis_index("expert"))
    rows = part.shape[1]
    for i in range(2):
        apart = jnp.bitwise_xor(2 * pl.program_id(0) + i, x)
        slot = jnp.where(apart == 0, 0, jnp.where(apart == 2, 3, jnp.where(apart == first, 2, 1)))
        part[slot] = product[i * rows : (i + 1) * rows]


def multiply_span(span, counts, activations, grads):
    _, _, _, slots, rows = activations.shape
    width = grads.shape[-1]
    part = (NX, rows // NX, width)
    return pl.pallas_call(
        functools.partial(span_kernel, span),
        grid_spec=pltpu.PrefetchScalarGridSpec(
            num_scalar_prefetch=1,
            grid=(2,),
            in_specs=[
                pl.BlockSpec((1, 1, 1, slots, rows // 2), lambda i, c: (0, 0, span, 0, i)),
                pl.BlockSpec((1, slots, width), lambda i, c: (span, 0, 0)),
            ],
            out_specs=pl.BlockSpec(part, lambda i, c: (0, 0, 0)),
            scratch_shapes=[pltpu.VMEM((slots, width), grads.dtype)],
        ),
        out_shape=jax.ShapeDtypeStruct(part, jnp.float32),
        compiler_params=pltpu.CompilerParams(vmem_limit_bytes=VMEM_BYTES),
        cost_estimate=cost(2 * slots * rows * width, 6 << 20),
    )(counts, activations, grads)


def narrow(values, scale):
    return (values * scale).astype(jnp.float16)


def widen(values, scale):
    return values.astype(jnp.float32) * (1.0 / scale)


def after(value, *earlier):
    return lax.optimization_barrier((value, *earlier))[0]


def piece(array, index):
    rows = array.shape[0] // NY
    return lax.dynamic_slice_in_dim(array, index * rows, rows, 0)


def exchange_y(quarter, y):
    out = [narrow(piece(quarter, y ^ k), Y_SCALE) for k in range(1, NY)]
    return out, [send(block, over_y(k)) for k, block in enumerate(out, 1)]


def local(activations, out_grads, counts, first_moment, second_moment):
    y = lax.axis_index("dp") % NY
    live = counts[0, 0]
    grads = lax.all_gather(out_grads[0, 0], "expert", axis=1, tiled=True)

    other = multiply_span(1, live, activations, grads)
    other_half = narrow(other[2:], X_SCALE)
    other_got = send(other_half, over_x_first)
    own = multiply_span(0, live, activations, after(grads, other_half))
    own_half = narrow(own[2:], X_SCALE)
    own_got = send(own_half, over_x_first)
    other_pass = narrow(after(other[1], own_half) + widen(other_got[1], X_SCALE), X_SCALE)
    other_last = send(other_pass, over_x_second)
    own_pass = narrow(after(own[1], other_pass) + widen(own_got[1], X_SCALE), X_SCALE)
    own_last = send(own_pass, over_x_second)

    other_x = after(other[0], own_pass) + widen(other_got[0], X_SCALE) + widen(other_last, X_SCALE)
    other_out, other_in = exchange_y(other_x, y)
    own_x = after(own[0], *other_out) + widen(own_got[0], X_SCALE) + widen(own_last, X_SCALE)
    own_out, own_in = exchange_y(own_x, y)
    other_rows = piece(after(other_x, *own_out), y) + sum(widen(block, Y_SCALE) for block in other_in)
    mirror_rows = send(narrow(other_rows, Z_SCALE), mirrored)
    grad = piece(own_x, y) + sum(widen(block, Y_SCALE) for block in own_in)
    grad = (grad + widen(mirror_rows, Z_SCALE))[None, None]
    new_first = 0.9 * first_moment + 0.1 * grad
    new_second = 0.95 * second_moment + 0.05 * grad * grad
    direction = new_first / (jnp.sqrt(new_second) + 1e-08)
    return (new_first, new_second, direction)


def solution(mesh):
    state = P("pipe", "expert", "dp", None)
    return jax.shard_map(
        local,
        mesh=mesh,
        in_specs=(
            P("dp", "pipe", None, None, "expert"),
            P("dp", "pipe", None, "expert", None),
            P("dp", "pipe", None),
            state,
            state,
        ),
        out_specs=(state, state, state),
        check_vma=False,
    )
```

```python
import functools

import jax
import jax.numpy as jnp
from jax import lax
from jax.experimental import pallas as pl
from jax.experimental.pallas import tpu as pltpu
from jax.sharding import PartitionSpec as P

AXES = ("dp", "pipe", "expert")
NX, NY = 4, 4
X_SCALE, Y_SCALE, Z_SCALE = 64.0, 32.0, 8.0
VMEM_BYTES = 32 << 20


def x_steps(expert):
    first = 1 + 2 * (expert % 2)
    return first, 4 - first


def over_x(step):
    return lambda dp, pipe, expert: (dp ^ x_steps(expert)[step] * NY, pipe, expert)


def over_y(bits):
    return lambda dp, pipe, expert: (dp ^ bits, pipe, expert)


def mirrored(dp, pipe, expert):
    return dp, lax.axis_size("pipe") - 1 - pipe, expert


def send(block, to):
    sizes = [lax.axis_size(name) for name in AXES]

    def flat(dp, pipe, expert):
        return (dp * sizes[1] + pipe) * sizes[2] + expert

    pairs = [
        (flat(d, p, e), flat(*to(d, p, e)))
        for d in range(sizes[0])
        for p in range(sizes[1])
        for e in range(sizes[2])
    ]
    return lax.ppermute(block, AXES, pairs)


def transposed_dot(a, b):
    return lax.dot_general(a, b, (((0,), (0,)), ((), ())), preferred_element_type=jnp.float32)


def cost(flops, read_and_written):
    return pl.CostEstimate(flops=flops, bytes_accessed=read_and_written, transcendentals=0)


def span_kernel(span, counts, acts, grads, part):
    live = lax.broadcasted_iota(jnp.int32, grads.shape[1:], 0) < counts[span]
    masked = jnp.where(live, grads[span].astype(jnp.float32), 0.0).astype(grads.dtype)
    dp = lax.axis_index("dp")
    x, y = dp // NY, lax.rem(dp, NY)
    first, _ = x_steps(lax.axis_index("expert"))
    rows = part.shape[2]
    for pair in range(NX // 2):
        columns = slice(pair * 4 * NY * rows, (pair + 1) * 4 * NY * rows)
        product = transposed_dot(acts[0, 0, span, :, columns], masked)
        for i in range(2):
            apart = jnp.bitwise_xor(2 * pair + i, x)
            slot = jnp.where(
                apart == 0, 0, jnp.where(apart == 2, 3, jnp.where(apart == first, 2, 1))
            )
            for j in range(NY):
                start = (i * NY + j) * 2 * rows
                halves = [product[start + k * rows : start + (k + 1) * rows] for k in range(2)]
                part[slot, jnp.bitwise_xor(j, y)] = jnp.concatenate(halves, axis=1)


def multiply_span(span, counts, activations, grads):
    _, _, _, slots, rows = activations.shape
    width = grads.shape[-1]
    vmem = pl.BlockSpec(memory_space=pltpu.VMEM)
    return pl.pallas_call(
        functools.partial(span_kernel, span),
        in_specs=[pl.BlockSpec(memory_space=pltpu.SMEM), vmem, vmem],
        out_specs=vmem,
        out_shape=jax.ShapeDtypeStruct((NX, NY, rows // (2 * NX * NY), 2 * width), jnp.float32),
        compiler_params=pltpu.CompilerParams(vmem_limit_bytes=VMEM_BYTES),
        cost_estimate=cost(2 * slots * rows * width, 6 << 20),
    )(counts, activations, grads)


def narrow(values, scale):
    return (values * scale).astype(jnp.float16)


def widen(values, scale):
    return values.astype(jnp.float32) * (1.0 / scale)


def after(value, *earlier):
    return lax.optimization_barrier((value, *earlier))[0]


def local(activations, out_grads, counts, first_moment, second_moment):
    live = counts[0, 0]
    grads = lax.all_gather(out_grads[0, 0], "expert", axis=1, tiled=True)

    other = multiply_span(1, live, activations, grads)
    other_out = narrow(other[2:], X_SCALE)
    other_in = send(other_out, over_x(0))
    own = multiply_span(0, live, activations, after(grads, other_out))
    own_out = narrow(own[2:], X_SCALE)
    own_in = send(own_out, over_x(0))
    other_pass = narrow(after(other[1], own_out) + widen(other_in[1], X_SCALE), X_SCALE)
    other_last = send(other_pass, over_x(1))
    own_pass = narrow(after(own[1], other_pass) + widen(own_in[1], X_SCALE), X_SCALE)
    own_last = send(own_pass, over_x(1))

    other = after(other[0], own_pass) + widen(other_in[0], X_SCALE) + widen(other_last, X_SCALE)
    other_out = [narrow(other[k], Y_SCALE) for k in range(1, NY)]
    other_in = [send(block, over_y(k)) for k, block in enumerate(other_out, 1)]
    own = after(own[0], *other_out) + widen(own_in[0], X_SCALE) + widen(own_last, X_SCALE)
    own_out = [narrow(own[k], Y_SCALE) for k in range(1, NY)]
    own_in = [send(block, over_y(k)) for k, block in enumerate(own_out, 1)]
    other = after(other[0], *own_out) + sum(widen(block, Y_SCALE) for block in other_in)
    from_mirror = send(narrow(other, Z_SCALE), mirrored)
    grad = own[0] + sum(widen(block, Y_SCALE) for block in own_in) + widen(from_mirror, Z_SCALE)
    width = out_grads.shape[-1]
    grad = jnp.concatenate([grad[:, :width], grad[:, width:]])[None, None]
    new_first = 0.9 * first_moment + 0.1 * grad
    new_second = 0.95 * second_moment + 0.05 * grad * grad
    direction = new_first / (jnp.sqrt(new_second) + 1e-08)
    return (new_first, new_second, direction)


def solution(mesh):
    state = P("pipe", "expert", "dp", None)
    return jax.shard_map(
        local,
        mesh=mesh,
        in_specs=(
            P("dp", "pipe", None, None, "expert"),
            P("dp", "pipe", None, "expert", None),
            P("dp", "pipe", None),
            state,
            state,
        ),
        out_specs=(state, state, state),
        check_vma=False,
    )
```

```python
import functools

import jax
import jax.numpy as jnp
from jax import lax
from jax.experimental import pallas as pl
from jax.experimental.pallas import tpu as pltpu
from jax.sharding import PartitionSpec as P

AXES = ("dp", "pipe", "expert")
NX, NY = 4, 4
X_SCALE, Y_SCALE, Z_SCALE = 64.0, 32.0, 8.0
VMEM_BYTES = 32 << 20


def x_steps(expert):
    first = 1 + 2 * (expert % 2)
    return first, 4 - first


def over_x(step):
    return lambda dp, pipe, expert: (dp ^ x_steps(expert)[step] * NY, pipe, expert)


def over_y(bits):
    return lambda dp, pipe, expert: (dp ^ bits, pipe, expert)


def mirrored(dp, pipe, expert):
    return dp, lax.axis_size("pipe") - 1 - pipe, expert


def send(block, to):
    sizes = [lax.axis_size(name) for name in AXES]

    def flat(dp, pipe, expert):
        return (dp * sizes[1] + pipe) * sizes[2] + expert

    pairs = [
        (flat(d, p, e), flat(*to(d, p, e)))
        for d in range(sizes[0])
        for p in range(sizes[1])
        for e in range(sizes[2])
    ]
    return lax.ppermute(block, AXES, pairs)


def transposed_dot(a, b):
    return lax.dot_general(a, b, (((0,), (0,)), ((), ())), preferred_element_type=jnp.float32)


def cost(flops, read_and_written):
    return pl.CostEstimate(flops=flops, bytes_accessed=read_and_written, transcendentals=0)


def pair_columns(rows):
    width = 2 * rows // NX
    return [slice(start, start + width) for start in range(0, rows, width)]


def span_kernel(span, counts, acts, grads, part, acts_here, sems):
    fetches = []
    for pair, columns in enumerate(pair_columns(acts.shape[-1])):
        source = acts.at[0, 0, span, :, columns]
        fetches.append(pltpu.make_async_copy(source, acts_here.at[:, columns], sems.at[pair]))
        fetches[-1].start()
    shards, _, slots, width = grads.shape
    mine = grads[:, span].reshape(shards * slots, width)
    live = lax.broadcasted_iota(jnp.int32, mine.shape, 0) < counts[span]
    masked = jnp.where(live, mine.astype(jnp.float32), 0.0).astype(mine.dtype)
    dp = lax.axis_index("dp")
    x, y = dp // NY, lax.rem(dp, NY)
    first, _ = x_steps(lax.axis_index("expert"))
    rows = part.shape[2]
    for pair, columns in enumerate(pair_columns(acts.shape[-1])):
        fetches[pair].wait()
        product = transposed_dot(acts_here[:, columns], masked)
        for i in range(2):
            apart = jnp.bitwise_xor(2 * pair + i, x)
            slot = jnp.where(
                apart == 0, 0, jnp.where(apart == 2, 3, jnp.where(apart == first, 2, 1))
            )
            for j in range(NY):
                start = (i * NY + j) * 2 * rows
                halves = [product[start + k * rows : start + (k + 1) * rows] for k in range(2)]
                part[slot, jnp.bitwise_xor(j, y)] = jnp.concatenate(halves, axis=1)


def in_hbm(array):
    return pltpu.with_memory_space_constraint(array, pltpu.HBM)


def multiply_span(span, counts, activations, grads):
    _, _, _, slots, rows = activations.shape
    width = grads.shape[-1]
    vmem = pl.BlockSpec(memory_space=pltpu.VMEM)
    return pl.pallas_call(
        functools.partial(span_kernel, span),
        grid_spec=pltpu.PrefetchScalarGridSpec(
            num_scalar_prefetch=1,
            grid=(),
            in_specs=[pl.BlockSpec(memory_space=pltpu.HBM), vmem],
            out_specs=vmem,
            scratch_shapes=[
                pltpu.VMEM((slots, rows), activations.dtype),
                pltpu.SemaphoreType.DMA((NX // 2,)),
            ],
        ),
        out_shape=jax.ShapeDtypeStruct((NX, NY, rows // (2 * NX * NY), 2 * width), jnp.float32),
        compiler_params=pltpu.CompilerParams(vmem_limit_bytes=VMEM_BYTES),
        cost_estimate=cost(2 * slots * rows * width, 6 << 20),
    )(counts, in_hbm(activations), grads)


def narrow(values, scale):
    return (values * scale).astype(jnp.float16)


def widen(values, scale):
    return values.astype(jnp.float32) * (1.0 / scale)


def after(value, *earlier):
    return lax.optimization_barrier((value, *earlier))[0]


def local(activations, out_grads, counts, first_moment, second_moment):
    live = in_hbm(counts[0, 0])
    grads = lax.all_gather(out_grads[0, 0], "expert")

    other = multiply_span(1, live, activations, grads)
    other_out = narrow(other[2:], X_SCALE)
    other_in = send(other_out, over_x(0))
    own = multiply_span(0, live, activations, after(grads, other_out))
    own_out = narrow(own[2:], X_SCALE)
    own_in = send(own_out, over_x(0))
    other_pass = narrow(after(other[1], own_out) + widen(other_in[1], X_SCALE), X_SCALE)
    other_last = send(other_pass, over_x(1))
    own_pass = narrow(after(own[1], other_pass) + widen(own_in[1], X_SCALE), X_SCALE)
    own_last = send(own_pass, over_x(1))

    other = after(other[0], own_pass) + widen(other_in[0], X_SCALE) + widen(other_last, X_SCALE)
    other_out = [narrow(other[k], Y_SCALE) for k in range(1, NY)]
    other_in = [send(block, over_y(k)) for k, block in enumerate(other_out, 1)]
    own = after(own[0], *other_out) + widen(own_in[0], X_SCALE) + widen(own_last, X_SCALE)
    own_out = [narrow(own[k], Y_SCALE) for k in range(1, NY)]
    own_in = [send(block, over_y(k)) for k, block in enumerate(own_out, 1)]
    other = after(other[0], *own_out) + sum(widen(block, Y_SCALE) for block in other_in)
    from_mirror = send(narrow(other, Z_SCALE), mirrored)
    grad = own[0] + sum(widen(block, Y_SCALE) for block in own_in) + widen(from_mirror, Z_SCALE)
    width = out_grads.shape[-1]
    grad = jnp.concatenate([grad[:, :width], grad[:, width:]])[None, None]
    new_first = 0.9 * first_moment + 0.1 * grad
    new_second = 0.95 * second_moment + 0.05 * grad * grad
    direction = new_first / (jnp.sqrt(new_second) + 1e-08)
    return (new_first, new_second, direction)


def solution(mesh):
    state = P("pipe", "expert", "dp", None)
    return jax.shard_map(
        local,
        mesh=mesh,
        in_specs=(
            P("dp", "pipe", None, None, "expert"),
            P("dp", "pipe", None, "expert", None),
            P("dp", "pipe", None),
            state,
            state,
        ),
        out_specs=(state, state, state),
        check_vma=False,
    )
```

```python
import functools

import jax
import jax.numpy as jnp
from jax import lax
from jax.experimental import pallas as pl
from jax.experimental.pallas import tpu as pltpu
from jax.sharding import PartitionSpec as P

AXES = ("dp", "pipe", "expert")
NX, NY = 4, 4
SCALES = (64.0, 64.0, 32.0, 16.0, 8.0)
VMEM_BYTES = 32 << 20


X_1, X_3, Y_1, LAST = 1 * NY, 3 * NY, 1, 2
ORDERS = (((X_3, Y_1, X_1), (Y_1, X_1, X_3)), ((X_1, Y_1, X_3), (X_3, X_1, Y_1)))


def step(span, number):
    def to(dp, pipe, expert):
        return dp ^ (*ORDERS[span][expert % 2], LAST)[number], pipe, expert

    return to


def mirrored(dp, pipe, expert):
    return dp, lax.axis_size("pipe") - 1 - pipe, expert


def send(block, to):
    sizes = [lax.axis_size(name) for name in AXES]

    def flat(dp, pipe, expert):
        return (dp * sizes[1] + pipe) * sizes[2] + expert

    pairs = [
        (flat(d, p, e), flat(*to(d, p, e)))
        for d in range(sizes[0])
        for p in range(sizes[1])
        for e in range(sizes[2])
    ]
    return lax.ppermute(block, AXES, pairs)


def transposed_dot(a, b):
    return lax.dot_general(a, b, (((0,), (0,)), ((), ())), preferred_element_type=jnp.float32)


def cost(flops, read_and_written):
    return pl.CostEstimate(flops=flops, bytes_accessed=read_and_written, transcendentals=0)


def pair_columns(rows):
    width = 2 * rows // NX
    return [slice(start, start + width) for start in range(0, rows, width)]


def span_kernel(span, counts, acts, grads, part, acts_here, sems):
    fetches = []
    for pair, columns in enumerate(pair_columns(acts.shape[-1])):
        source = acts.at[0, 0, span, :, columns]
        fetches.append(pltpu.make_async_copy(source, acts_here.at[:, columns], sems.at[pair]))
        fetches[-1].start()
    shards, _, slots, width = grads.shape
    mine = grads[:, span].reshape(shards * slots, width)
    live = lax.broadcasted_iota(jnp.int32, mine.shape, 0) < counts[span]
    masked = jnp.where(live, mine.astype(jnp.float32), 0.0).astype(mine.dtype)
    dp, expert = lax.axis_index("dp"), lax.axis_index("expert")
    x, y = dp // NY, lax.rem(dp, NY)
    core_0, core_1 = ([8 >> order.index(part) for part in (X_1, X_3, Y_1)] for order in ORDERS[span])
    x_1, x_3, y_1 = (jnp.where(lax.rem(expert, 2) == 0, p, q) for p, q in zip(core_0, core_1))
    x_places, y_places = [], []
    for i in range(NX):
        apart = jnp.bitwise_xor(i, x)
        x_place = jnp.where((apart == 1) | (apart == 2), x_1, 0)
        x_places.append(x_place + jnp.where((apart == 3) | (apart == 2), x_3, 0))
        apart = jnp.bitwise_xor(i, y)
        y_places.append(lax.rem(apart, 2) * y_1 + apart // 2)
    rows = part.shape[1]
    for pair, columns in enumerate(pair_columns(acts.shape[-1])):
        fetches[pair].wait()
        product = transposed_dot(acts_here[:, columns], masked)
        for i in range(2):
            for j in range(NY):
                start = (i * NY + j) * 2 * rows
                halves = [product[start + k * rows : start + (k + 1) * rows] for k in range(2)]
                part[x_places[2 * pair + i] + y_places[j]] = jnp.concatenate(halves, axis=1)


def in_hbm(array):
    return pltpu.with_memory_space_constraint(array, pltpu.HBM)


def multiply_span(span, counts, activations, grads):
    _, _, _, slots, rows = activations.shape
    width = grads.shape[-1]
    vmem = pl.BlockSpec(memory_space=pltpu.VMEM)
    return pl.pallas_call(
        functools.partial(span_kernel, span),
        grid_spec=pltpu.PrefetchScalarGridSpec(
            num_scalar_prefetch=1,
            grid=(),
            in_specs=[pl.BlockSpec(memory_space=pltpu.HBM), vmem],
            out_specs=vmem,
            scratch_shapes=[
                pltpu.VMEM((slots, rows), activations.dtype),
                pltpu.SemaphoreType.DMA((NX // 2,)),
            ],
        ),
        out_shape=jax.ShapeDtypeStruct((NX * NY, rows // (2 * NX * NY), 2 * width), jnp.float32),
        compiler_params=pltpu.CompilerParams(vmem_limit_bytes=VMEM_BYTES),
        cost_estimate=cost(2 * slots * rows * width, 6 << 20),
    )(counts, in_hbm(activations), grads)


def narrow(values, scale):
    return (values * scale).astype(jnp.float16)


def widen(values, scale):
    return values.astype(jnp.float32) * (1.0 / scale)


def after(value, *earlier):
    return lax.optimization_barrier((value, *earlier))[0]


def local(activations, out_grads, counts, first_moment, second_moment):
    live = in_hbm(counts[0, 0])
    grads = lax.all_gather(out_grads[0, 0], "expert")

    other = multiply_span(1, live, activations, grads)
    other_out = narrow(other[8:], SCALES[0])
    other_in = send(other_out, step(1, 0))
    own = multiply_span(0, live, activations, after(grads, other_out))
    own_out = narrow(own[8:], SCALES[0])
    own_in = send(own_out, step(0, 0))
    for number, kept in ((1, 8), (2, 4), (3, 2)):
        scale = SCALES[number - 1]
        other = after(other[:kept], own_out) + widen(other_in, scale)
        other_out = narrow(other[kept // 2 :], SCALES[number])
        other_in = send(other_out, step(1, number))
        own = after(own[:kept], other_out) + widen(own_in, scale)
        own_out = narrow(own[kept // 2 :], SCALES[number])
        own_in = send(own_out, step(0, number))

    other = after(other[:1], own_out) + widen(other_in, SCALES[3])
    from_mirror = send(narrow(other, SCALES[4]), mirrored)
    grad = (own[:1] + widen(own_in, SCALES[3]) + widen(from_mirror, SCALES[4]))[0]
    width = out_grads.shape[-1]
    grad = jnp.concatenate([grad[:, :width], grad[:, width:]])[None, None]
    new_first = 0.9 * first_moment + 0.1 * grad
    new_second = 0.95 * second_moment + 0.05 * grad * grad
    direction = new_first / (jnp.sqrt(new_second) + 1e-08)
    return (new_first, new_second, direction)


def solution(mesh):
    state = P("pipe", "expert", "dp", None)
    return jax.shard_map(
        local,
        mesh=mesh,
        in_specs=(
            P("dp", "pipe", None, None, "expert"),
            P("dp", "pipe", None, "expert", None),
            P("dp", "pipe", None),
            state,
            state,
        ),
        out_specs=(state, state, state),
        check_vma=False,
    )
```

```python
import functools

import jax
import jax.numpy as jnp
from jax import lax
from jax.experimental import pallas as pl
from jax.experimental.pallas import tpu as pltpu
from jax.sharding import PartitionSpec as P

AXES = ("dp", "pipe", "expert")
NX, NY = 4, 4
SCALES = (64.0, 64.0, 32.0, 16.0, 8.0)
VMEM_BYTES = 32 << 20


X_1, X_3, Y_1, Y_2 = 1 * NY, 3 * NY, 1, 2
ORDERS = (
    ((X_3, X_1, Y_1, Y_2), (Y_1, X_3, X_1, Y_2)),
    ((X_1, Y_1, X_3, Y_2), (X_3, X_1, Y_1, Y_2)),
)


def step(span, *numbers):
    def to(dp, pipe, expert):
        for number in numbers:
            dp ^= ORDERS[span][expert % 2][number]
        return dp, pipe, expert

    return to


def mirrored(dp, pipe, expert):
    return dp, lax.axis_size("pipe") - 1 - pipe, expert


def send(block, to):
    sizes = [lax.axis_size(name) for name in AXES]

    def flat(dp, pipe, expert):
        return (dp * sizes[1] + pipe) * sizes[2] + expert

    pairs = [
        (flat(d, p, e), flat(*to(d, p, e)))
        for d in range(sizes[0])
        for p in range(sizes[1])
        for e in range(sizes[2])
    ]
    return lax.ppermute(block, AXES, pairs)


def transposed_dot(a, b):
    return lax.dot_general(a, b, (((0,), (0,)), ((), ())), preferred_element_type=jnp.float32)


def cost(flops, read_and_written):
    return pl.CostEstimate(flops=flops, bytes_accessed=read_and_written, transcendentals=0)


def pair_columns(rows):
    width = 2 * rows // NX
    return [slice(start, start + width) for start in range(0, rows, width)]


def span_kernel(span, counts, acts, grads, part, acts_here, sems):
    fetches = []
    for pair, columns in enumerate(pair_columns(acts.shape[-1])):
        source = acts.at[0, 0, span, :, columns]
        fetches.append(pltpu.make_async_copy(source, acts_here.at[:, columns], sems.at[pair]))
        fetches[-1].start()
    shards, _, slots, width = grads.shape
    mine = grads[:, span].reshape(shards * slots, width)
    live = lax.broadcasted_iota(jnp.int32, mine.shape, 0) < counts[span]
    masked = jnp.where(live, mine.astype(jnp.float32), 0.0).astype(mine.dtype)
    dp, expert = lax.axis_index("dp"), lax.axis_index("expert")
    x, y = dp // NY, lax.rem(dp, NY)
    places = ([8 >> order.index(part) for part in (X_1, X_3, Y_1, Y_2)] for order in ORDERS[span])
    is_0 = lax.rem(expert, 2) == 0
    x_1, x_3, y_1, y_2 = (jnp.where(is_0, p, q) for p, q in zip(*places))
    x_places, y_places = [], []
    for i in range(NX):
        apart = jnp.bitwise_xor(i, x)
        x_place = jnp.where((apart == 1) | (apart == 2), x_1, 0)
        x_places.append(x_place + jnp.where((apart == 3) | (apart == 2), x_3, 0))
        apart = jnp.bitwise_xor(i, y)
        y_places.append(lax.rem(apart, 2) * y_1 + apart // 2 * y_2)
    rows = part.shape[1]
    for pair, columns in enumerate(pair_columns(acts.shape[-1])):
        fetches[pair].wait()
        product = transposed_dot(acts_here[:, columns], masked)
        for i in range(2):
            for j in range(NY):
                start = (i * NY + j) * 2 * rows
                halves = [product[start + k * rows : start + (k + 1) * rows] for k in range(2)]
                part[x_places[2 * pair + i] + y_places[j]] = jnp.concatenate(halves, axis=1)


def in_hbm(array):
    return pltpu.with_memory_space_constraint(array, pltpu.HBM)


def multiply_span(span, counts, activations, grads):
    _, _, _, slots, rows = activations.shape
    width = grads.shape[-1]
    vmem = pl.BlockSpec(memory_space=pltpu.VMEM)
    return pl.pallas_call(
        functools.partial(span_kernel, span),
        grid_spec=pltpu.PrefetchScalarGridSpec(
            num_scalar_prefetch=1,
            grid=(),
            in_specs=[pl.BlockSpec(memory_space=pltpu.HBM), vmem],
            out_specs=vmem,
            scratch_shapes=[
                pltpu.VMEM((slots, rows), activations.dtype),
                pltpu.SemaphoreType.DMA((NX // 2,)),
            ],
        ),
        out_shape=jax.ShapeDtypeStruct((NX * NY, rows // (2 * NX * NY), 2 * width), jnp.float32),
        compiler_params=pltpu.CompilerParams(vmem_limit_bytes=VMEM_BYTES),
        cost_estimate=cost(2 * slots * rows * width, 6 << 20),
    )(counts, in_hbm(activations), grads)


def narrow(values, scale):
    return (values * scale).astype(jnp.float16)


def widen(values, scale):
    return values.astype(jnp.float32) * (1.0 / scale)


def after(value, *earlier):
    return lax.optimization_barrier((value, *earlier))[0]


def local(activations, out_grads, counts, first_moment, second_moment):
    live = in_hbm(counts[0, 0])
    grads = lax.all_gather(out_grads[0, 0], "expert")

    def direct(part, span, *earlier):
        part = after(part, *earlier)
        out = [narrow(part[k], SCALES[2]) for k in (1, 2, 3)]
        partners = (3,), (2,), (2, 3)
        return out, part[0], [send(block, step(span, *to)) for block, to in zip(out, partners)]

    def total(kept, blocks):
        return kept + sum(widen(block, SCALES[2]) for block in blocks)

    other = multiply_span(1, live, activations, grads)
    other_out = narrow(other[8:], SCALES[0])
    other_in = send(other_out, step(1, 0))
    own = multiply_span(0, live, activations, after(grads, other_out))
    own_out = narrow(own[8:], SCALES[0])
    own_in = send(own_out, step(0, 0))
    other = after(other[:8], own_out) + widen(other_in, SCALES[0])
    other_out = narrow(other[4:], SCALES[1])
    other_in = send(other_out, step(1, 1))
    own = after(own[:8], other_out) + widen(own_in, SCALES[0])
    own_out = narrow(own[4:], SCALES[1])
    own_in = send(own_out, step(0, 1))
    other = after(other[:4], own_out) + widen(other_in, SCALES[1])
    other_out, other, other_in = direct(other, 1)
    own = after(own[:4], *other_out) + widen(own_in, SCALES[1])
    own_out, own, own_in = direct(own, 0)

    other = total(after(other, *own_out), other_in)
    from_mirror = send(narrow(other, SCALES[4]), mirrored)
    grad = total(own, own_in) + widen(from_mirror, SCALES[4])
    width = out_grads.shape[-1]
    grad = jnp.concatenate([grad[:, :width], grad[:, width:]])[None, None]
    new_first = 0.9 * first_moment + 0.1 * grad
    new_second = 0.95 * second_moment + 0.05 * grad * grad
    direction = new_first / (jnp.sqrt(new_second) + 1e-08)
    return (new_first, new_second, direction)


def solution(mesh):
    state = P("pipe", "expert", "dp", None)
    return jax.shard_map(
        local,
        mesh=mesh,
        in_specs=(
            P("dp", "pipe", None, None, "expert"),
            P("dp", "pipe", None, "expert", None),
            P("dp", "pipe", None),
            state,
            state,
        ),
        out_specs=(state, state, state),
        check_vma=False,
    )
```

```python
import functools

import jax
import jax.numpy as jnp
from jax import lax
from jax.experimental import pallas as pl
from jax.experimental.pallas import tpu as pltpu
from jax.sharding import PartitionSpec as P

AXES = ("dp", "pipe", "expert")
NX, NY = 4, 4
SCALES = (64.0, 64.0, 32.0, 16.0, 8.0)
VMEM_BYTES = 32 << 20


X_1, X_3, Y_1, Y_2 = 1 * NY, 3 * NY, 1, 2
ORDERS = (
    ((X_3, X_1, Y_1, Y_2), (Y_1, X_3, X_1, Y_2)),
    ((X_1, Y_1, X_3, Y_2), (X_3, X_1, Y_2, Y_1)),
)


def step(span, *numbers):
    def to(dp, pipe, expert):
        for number in numbers:
            dp ^= ORDERS[span][expert % 2][number]
        return dp, pipe, expert

    return to


def mirrored(dp, pipe, expert):
    return dp, lax.axis_size("pipe") - 1 - pipe, expert


def send(block, to):
    sizes = [lax.axis_size(name) for name in AXES]

    def flat(dp, pipe, expert):
        return (dp * sizes[1] + pipe) * sizes[2] + expert

    pairs = [
        (flat(d, p, e), flat(*to(d, p, e)))
        for d in range(sizes[0])
        for p in range(sizes[1])
        for e in range(sizes[2])
    ]
    return lax.ppermute(block, AXES, pairs)


def transposed_dot(a, b):
    return lax.dot_general(a, b, (((0,), (0,)), ((), ())), preferred_element_type=jnp.float32)


def cost(flops, read_and_written):
    return pl.CostEstimate(flops=flops, bytes_accessed=read_and_written, transcendentals=0)


def pair_columns(rows):
    width = 2 * rows // NX
    return [slice(start, start + width) for start in range(0, rows, width)]


def span_kernel(span, counts, acts, grads, part, acts_here, sems):
    fetches = []
    for pair, columns in enumerate(pair_columns(acts.shape[-1])):
        source = acts.at[0, 0, span, :, columns]
        fetches.append(pltpu.make_async_copy(source, acts_here.at[:, columns], sems.at[pair]))
        fetches[-1].start()
    shards, _, slots, width = grads.shape
    mine = grads[:, span].reshape(shards * slots, width)
    live = lax.broadcasted_iota(jnp.int32, mine.shape, 0) < counts[span]
    masked = jnp.where(live, mine.astype(jnp.float32), 0.0).astype(mine.dtype)
    dp, expert = lax.axis_index("dp"), lax.axis_index("expert")
    x, y = dp // NY, lax.rem(dp, NY)
    places = ([8 >> order.index(part) for part in (X_1, X_3, Y_1, Y_2)] for order in ORDERS[span])
    is_0 = lax.rem(expert, 2) == 0
    x_1, x_3, y_1, y_2 = (jnp.where(is_0, p, q) for p, q in zip(*places))
    x_places, y_places = [], []
    for i in range(NX):
        apart = jnp.bitwise_xor(i, x)
        x_place = jnp.where((apart == 1) | (apart == 2), x_1, 0)
        x_places.append(x_place + jnp.where((apart == 3) | (apart == 2), x_3, 0))
        apart = jnp.bitwise_xor(i, y)
        y_places.append(lax.rem(apart, 2) * y_1 + apart // 2 * y_2)
    rows = part.shape[1]
    for pair, columns in enumerate(pair_columns(acts.shape[-1])):
        fetches[pair].wait()
        product = transposed_dot(acts_here[:, columns], masked)
        for i in range(2):
            for j in range(NY):
                start = (i * NY + j) * 2 * rows
                halves = [product[start + k * rows : start + (k + 1) * rows] for k in range(2)]
                part[x_places[2 * pair + i] + y_places[j]] = jnp.concatenate(halves, axis=1)


def in_hbm(array):
    return pltpu.with_memory_space_constraint(array, pltpu.HBM)


def multiply_span(span, counts, activations, grads):
    _, _, _, slots, rows = activations.shape
    width = grads.shape[-1]
    vmem = pl.BlockSpec(memory_space=pltpu.VMEM)
    return pl.pallas_call(
        functools.partial(span_kernel, span),
        grid_spec=pltpu.PrefetchScalarGridSpec(
            num_scalar_prefetch=1,
            grid=(),
            in_specs=[pl.BlockSpec(memory_space=pltpu.HBM), vmem],
            out_specs=vmem,
            scratch_shapes=[
                pltpu.VMEM((slots, rows), activations.dtype),
                pltpu.SemaphoreType.DMA((NX // 2,)),
            ],
        ),
        out_shape=jax.ShapeDtypeStruct((NX * NY, rows // (2 * NX * NY), 2 * width), jnp.float32),
        compiler_params=pltpu.CompilerParams(vmem_limit_bytes=VMEM_BYTES),
        cost_estimate=cost(2 * slots * rows * width, 6 << 20),
    )(counts, in_hbm(activations), grads)


def narrow(values, scale):
    return (values * scale).astype(jnp.float16)


def widen(values, scale):
    return values.astype(jnp.float32) * (1.0 / scale)


def after(value, *earlier):
    return lax.optimization_barrier((value, *earlier))[0]


def local(activations, out_grads, counts, first_moment, second_moment):
    live = in_hbm(counts[0, 0])
    grads = lax.all_gather(out_grads[0, 0], "expert")

    def direct(part, span, *earlier):
        part = after(part, *earlier)
        out = [narrow(part[k], SCALES[2]) for k in (1, 2, 3)]
        partners = (3,), (2,), (2, 3)
        return out, part[0], [send(block, step(span, *to)) for block, to in zip(out, partners)]

    def total(kept, blocks):
        return kept + sum(widen(block, SCALES[2]) for block in blocks)

    other = multiply_span(1, live, activations, grads)
    other_out = narrow(other[8:], SCALES[0])
    other_in = send(other_out, step(1, 0))
    own = multiply_span(0, live, activations, after(grads, other_out))
    own_out = narrow(own[8:], SCALES[0])
    own_in = send(own_out, step(0, 0))
    other = after(other[:8], own_out) + widen(other_in, SCALES[0])
    other_out = narrow(other[4:], SCALES[1])
    other_in = send(other_out, step(1, 1))
    own = after(own[:8], other_out) + widen(own_in, SCALES[0])
    own_out = narrow(own[4:], SCALES[1])
    own_in = send(own_out, step(0, 1))
    other = after(other[:4], own_out) + widen(other_in, SCALES[1])
    other_out, other, other_in = direct(other, 1)
    own = after(own[:4], *other_out) + widen(own_in, SCALES[1])
    own_out, own, own_in = direct(own, 0)

    other = total(after(other, *own_out), other_in)
    from_mirror = send(narrow(other, SCALES[4]), mirrored)
    own = lax.optimization_barrier(total(own, own_in))
    grad = own + widen(from_mirror, SCALES[4])
    width = out_grads.shape[-1]
    grad = jnp.concatenate([grad[:, :width], grad[:, width:]])[None, None]
    new_first = 0.9 * first_moment + 0.1 * grad
    new_second = 0.95 * second_moment + 0.05 * grad * grad
    direction = new_first / (jnp.sqrt(new_second) + 1e-08)
    return (new_first, new_second, direction)


def solution(mesh):
    state = P("pipe", "expert", "dp", None)
    return jax.shard_map(
        local,
        mesh=mesh,
        in_specs=(
            P("dp", "pipe", None, None, "expert"),
            P("dp", "pipe", None, "expert", None),
            P("dp", "pipe", None),
            state,
            state,
        ),
        out_specs=(state, state, state),
        check_vma=False,
    )
```
